32 devices in a mesh: freq: 4 (over y, x), cell: 8 (over z, core).
Axes of the slice: x: 2, y: 2, z: 4, core: 2. Of those that a mesh axis runs over, the one named last changes fastest.
Arguments:
- snapshots: bfloat16 [8, 2, 16, 512], P('freq', None, 'cell'), may hold values from -6 to 6
- previous: float32 [8, 2, 512, 512], P('freq', None, 'cell'), may hold values from -40 to 40, as said below
- replicas: bfloat16 [8, 2, 8192, 512], P('freq', None, 'cell'), may hold values from -1 to 1, as said below
Outputs:
- power: float32 [8192], P('cell')
- csdm: float32 [8, 2, 512, 512], P('freq', None, 'cell')
The draws below stay inside these ranges and needn't reach their ends.
Inputs may be any that keep to these rules, and one draw needn't show every extreme that they name: `previous`: for every frequency the real part is symmetric with a positive diagonal and the imaginary part is antisymmetric. `replicas`: every entry of a replica vector has modulus 1 / sqrt(512) up to bfloat16 rounding.
All inputs are finite; a program needn't handle non-finite values.
Results may differ from the reference program's by a relative error of at most 0.0003.
Values may be sent and summed in bfloat16 or wider, within the bound.
A program may use at most 64 MiB of HBM per device.

```python
import math
import jax
import jax.numpy as jnp
from jax import lax

M = 512
FREQS = 8
SNAPS = 16
CELLS = 8192


def source_field(key):
    key_phase, key_cells = jax.random.split(key)
    phases = jax.random.uniform(key_phase, (FREQS, M, M), jnp.float32, -math.pi, math.pi)
    planted = jax.random.permutation(key_cells, CELLS)[:min(M // 4, CELLS // 2)]
    return (phases, planted)


def draw_previous(key, part):
    phases, planted = source_field(key)
    key = jax.random.fold_in(key, 11)
    key_amp, key_scale, key_noise = jax.random.split(key, 3)
    top = math.log(10.0)
    noise = jax.random.uniform(key_noise, (FREQS, M), jnp.float32, 0.1, 0.4)
    amplitude = jnp.exp(jax.random.uniform(key_amp, (FREQS, M), jnp.float32, math.log(0.2), math.log(2.0)))
    scales = jnp.exp(0.5 * jax.random.uniform(key_scale, (FREQS, M), jnp.float32, 0.0, top))
    norm = 1.0 / math.sqrt(M)
    cos_vec = jnp.cos(phases) * norm
    sin_vec = jnp.sin(phases) * norm
    weighted_cos = cos_vec * amplitude[:, :, None]
    weighted_sin = sin_vec * amplitude[:, :, None]
    hp = lax.Precision.HIGHEST
    real_part = jnp.einsum('fpi,fpj->fij', weighted_cos, cos_vec, precision=hp) + jnp.einsum('fpi,fpj->fij', weighted_sin, sin_vec, precision=hp)
    imag_part = jnp.einsum('fpi,fpj->fij', weighted_sin, cos_vec, precision=hp) - jnp.einsum('fpi,fpj->fij', weighted_cos, sin_vec, precision=hp)
    real_sym = 0.5 * (real_part + jnp.swapaxes(real_part, 1, 2)) + jnp.eye(M, dtype=jnp.float32)[None] * noise[:, None, :]
    imag_anti = 0.5 * (imag_part - jnp.swapaxes(imag_part, 1, 2))
    outer = scales[:, :, None] * scales[:, None, :]
    return jnp.stack([real_sym * outer, imag_anti * outer], axis=1)


def draw_replicas(key, part):
    phases, planted = source_field(key)
    key = jax.random.fold_in(key, 23)
    base = jax.random.uniform(key, (FREQS, CELLS, M), jnp.float32, -math.pi, math.pi)
    count = planted.shape[0]
    base = base.at[:, planted, :].set(phases[:, :count, :])
    norm = 1.0 / math.sqrt(M)
    return jnp.stack([jnp.cos(base) * norm, jnp.sin(base) * norm], axis=1).astype(jnp.bfloat16)


def level_of(key, extent, cuts, least, top_value):
    def one(position, parts):
        heights = jax.random.uniform(jax.random.fold_in(jax.random.fold_in(key, 6), position), (parts,), jnp.float32, least / len(cuts), top_value / len(cuts))
        return jnp.repeat(jnp.exp(heights), extent[position] // parts).reshape((-1,) + (1,) * (len(extent) - position - 1))

    level = one(*cuts[0])
    for cut in cuts[1:]:
        level = level * one(*cut)
    return level


def scatter_about(own_key, shape, width, limit, pieces=(), kind=jnp.bfloat16):
    array = width * jax.random.normal(own_key, shape, jnp.float32)
    if pieces:
        array = array * level_of(own_key, shape, pieces, -0.22, 0.18)
    return jnp.clip(array, -limit, limit).astype(kind)


def setup_inputs(seed: int = 0) -> dict:
    streams_of = jax.random.split(jax.random.key(seed), 4)
    snapshots = scatter_about(streams_of[0], (FREQS, 2, SNAPS, M), 1.0, 6.0, ((0, 4), (2, 8)))
    previous = draw_previous(jax.random.fold_in(streams_of[3], 71), 0)
    replicas = draw_replicas(jax.random.fold_in(streams_of[3], 71), 0)
    return dict(snapshots=snapshots, previous=previous, replicas=replicas)


def score_one(items):
    real_rep, imag_rep, real_mat, imag_mat, trace_val = items
    hp = lax.Precision.HIGHEST
    real_rep = real_rep.astype(jnp.float32)
    imag_rep = imag_rep.astype(jnp.float32)
    yr = jnp.dot(real_rep, real_mat.T, precision=hp) - jnp.dot(imag_rep, imag_mat.T, precision=hp)
    yi = jnp.dot(imag_rep, real_mat.T, precision=hp) + jnp.dot(real_rep, imag_mat.T, precision=hp)
    bart = jnp.sum(real_rep * yr + imag_rep * yi, axis=1)
    return bart / trace_val


def reference(snapshots, previous, replicas):
    real_snap = snapshots[:, 0].astype(jnp.float32)
    imag_snap = snapshots[:, 1].astype(jnp.float32)
    hp = lax.Precision.HIGHEST
    cross_re = jnp.einsum("fsi,fsj->fij", real_snap, real_snap, precision=hp) + jnp.einsum("fsi,fsj->fij", imag_snap, imag_snap, precision=hp)
    cross_im = jnp.einsum("fsi,fsj->fij", imag_snap, real_snap, precision=hp) - jnp.einsum("fsi,fsj->fij", real_snap, imag_snap, precision=hp)
    cross = jnp.stack([cross_re, cross_im], axis=1)
    csdm = 0.8 * previous + (0.2 / SNAPS) * cross
    trace = jnp.trace(csdm[:, 0], axis1=1, axis2=2)
    ratios = lax.map(score_one, (replicas[:, 0], replicas[:, 1], csdm[:, 0], csdm[:, 1], trace))
    power = jnp.sum(ratios, axis=0) * (M / FREQS)
    return power, csdm
```

```python
import functools

import jax
import jax.numpy as jnp
from jax import lax
from jax.experimental import pallas as pl
from jax.experimental.pallas import tpu as pltpu
from jax.sharding import PartitionSpec as P

LINK = jnp.bfloat16
LIFT = 2.0**15.5
MESH = pl.DeviceIdType.MESH


def encode(x):
    x2 = x * x
    x4 = x2 * x2
    x8 = x4 * x4
    return jnp.where(x < 0, -x8, x8).astype(LINK)


def decode(y):
    y = y.astype(jnp.float32)
    root = jnp.exp(0.125 * jnp.log(jnp.maximum(jnp.abs(y), 1e-37)))
    return jnp.where(y < 0, -root, root)


def contract_rows(a, b):
    return lax.dot_general(
        a, b, (((0,), (0,)), ((), ())), preferred_element_type=jnp.float32
    )


def dot(a, b):
    return jnp.dot(a, b, preferred_element_type=jnp.float32)


def kernel(
    n, nf, snap_ref, prev_ref, rep_hbm, power_ref, csdm_ref,
    hbuf, mbuf, rep, cross_re, cross_im, high, low, lanes, slots,
    hsend, hrecv, fsend, frecv, msend, mrecv, gsend, grecv, psend, precv, rsem,
):
    F, _, S, M = snap_ref.shape
    R = prev_ref.shape[2]
    T = mbuf.shape[1]
    cells = rep.shape[2]
    chips = n // 2
    me = lax.axis_index("cell")
    fr = lax.axis_index("freq")
    chip, core = me // 2, lax.rem(me, 2)
    sib = chip * 2 + 1 - core

    loads = [pltpu.make_async_copy(rep_hbm.at[f], rep.at[f], rsem.at[f]) for f in range(F)]
    for f in range(F):
        loads[f].start()

    def ahead(d):
        return lax.rem(chip + d, chips) * 2 + core

    def behind(d):
        return lax.rem(chip + chips - d, chips) * 2 + core

    barrier = pltpu.get_barrier_semaphore()
    for d in range(1, chips):
        pl.semaphore_signal(barrier, inc=1, device_id=(fr, ahead(d)), device_id_type=MESH)
    pl.semaphore_signal(barrier, inc=1, device_id=(fr, sib), device_id_type=MESH)
    for d in range(1, nf):
        pl.semaphore_signal(barrier, inc=1, device_id=(lax.rem(fr + d, nf), me), device_id_type=MESH)

    row = lax.broadcasted_iota(jnp.int32, (T, M), 0)
    message = jnp.zeros((T, M), jnp.float32)
    for f in range(F):
        for p in range(2):
            values = snap_ref[f, p].astype(jnp.float32)
            for s in range(S):
                message = jnp.where(row == (f * 2 + p) * S + s, values[s : s + 1, :], message)
        h = prev_ref[f, 0] + prev_ref[f, 1]
        top = jnp.max(jnp.max(jnp.abs(h), axis=1, keepdims=True), axis=0, keepdims=True)
        scale = jnp.maximum(top, 1e-30).astype(jnp.bfloat16).astype(jnp.float32)
        hbuf[me, f] = encode(h * (LIFT / scale))
        message = jnp.where(row == 2 * S * F + f, scale, message)
    mbuf[me] = message.astype(jnp.bfloat16)

    def remote(ref, send, recv, to):
        return pltpu.make_async_remote_copy(
            src_ref=ref, dst_ref=ref, send_sem=send, recv_sem=recv,
            device_id=(fr, to), device_id_type=MESH,
        )

    pl.semaphore_wait(barrier, chips - 1 + 1 + nf - 1)

    sends = []
    for d in range(chips - 1, 0, -1):
        c = remote(mbuf.at[me], msend.at[d], mrecv.at[d], ahead(d))
        c.start()
        sends.append(c)
    c = remote(mbuf.at[me], msend.at[0], mrecv.at[0], sib)
    c.start()
    sends.append(c)
    for f in range(F):
        for d in range(chips - 1, 0, -1):
            c = remote(hbuf.at[me, f], hsend.at[f, d], hrecv.at[f, d], ahead(d))
            c.start()
            sends.append(c)
        c = remote(hbuf.at[me, f], hsend.at[f, 0], hrecv.at[f, 0], sib)
        c.start()
        sends.append(c)

    def other(d):
        return lax.rem(chip + chips - d, chips) * 2 + 1 - core

    for d in range(1, chips):
        ref = mbuf.at[behind(d)]
        remote(ref, msend.at[d], mrecv.at[d], sib).wait_recv()
        c = remote(ref, gsend.at[d], grecv.at[d], sib)
        c.start()
        sends.append(c)
    remote(mbuf.at[sib], msend.at[0], mrecv.at[0], sib).wait_recv()
    for d in range(1, chips):
        remote(mbuf.at[other(d)], gsend.at[d], grecv.at[d], sib).wait_recv()

    factor = 0.2 / (S * n)
    G = mbuf[...].reshape(n * T, M)
    a = lax.broadcasted_iota(jnp.int32, (n * T, n * T), 0)
    b = lax.broadcasted_iota(jnp.int32, (n * T, n * T), 1)
    place = lax.rem(a, T)
    used = place < 2 * S * F
    imag = lax.rem(place, 2 * S) >= S
    turn = jnp.where(used & imag & (b == a - S), 1.0, 0.0) - jnp.where(
        used & jnp.logical_not(imag) & (b == a + S), 1.0, 0.0
    )
    Z = dot(turn.astype(jnp.bfloat16), G).astype(jnp.bfloat16)
    spot = lax.rem(lax.broadcasted_iota(jnp.int32, (n * T, M), 0), T)
    Gf = G.astype(jnp.float32)
    mine = pl.ds(pl.multiple_of(me * R, R), R)
    for f in range(F):
        inside = (spot >= 2 * S * f) & (spot < 2 * S * (f + 1))
        X = jnp.where(inside, Gf, 0.0).astype(jnp.bfloat16)
        cross_re[f] = contract_rows(X, G) * factor
        cross_im[f] = contract_rows(X, Z) * factor
        csdm_ref[f, 0] = 0.8 * prev_ref[f, 0] + cross_re[f, mine]
        csdm_ref[f, 1] = 0.8 * prev_ref[f, 1] + cross_im[f, mine]

    step = min(512, cells)
    for f in range(F):
        for d in range(1, chips):
            ref = hbuf.at[behind(d), f]
            remote(ref, hsend.at[f, d], hrecv.at[f, d], sib).wait_recv()
            c = remote(ref, fsend.at[f, d], frecv.at[f, d], sib)
            c.start()
            sends.append(c)
    for f in range(F):
        remote(hbuf.at[sib, f], hsend.at[f, 0], hrecv.at[f, 0], sib).wait_recv()
        for d in range(1, chips):
            remote(hbuf.at[other(d), f], fsend.at[f, d], frecv.at[f, d], sib).wait_recv()
        trace = jnp.zeros((R, M), jnp.float32)
        ii = lax.broadcasted_iota(jnp.int32, (R, M), 0)
        jj = lax.broadcasted_iota(jnp.int32, (R, M), 1)
        for j in range(n):
            at = j * T + 2 * S * F + f
            back = Gf[at : at + 1, :] * (0.8 / LIFT)
            rows = slice(j * R, (j + 1) * R)
            full = decode(hbuf[j, f]) * back + (cross_re[f, rows] + cross_im[f, rows])
            trace = trace + jnp.where(jj == ii + j * R, full, 0.0)
            top = full.astype(jnp.bfloat16)
            high[rows, :] = top
            low[rows, :] = (full - top.astype(jnp.float32)).astype(jnp.bfloat16)
        total = jnp.sum(jnp.sum(trace, axis=0, keepdims=True), axis=1, keepdims=True)
        gain = (M / (F * nf)) / total
        loads[f].wait()
        for t in range(cells // step):
            at = slice(t * step, (t + 1) * step)
            u, v = rep[f, 0, at], rep[f, 1, at]
            yu = dot(u, high[...]) + dot(u, low[...])
            yv = dot(v, high[...]) + dot(v, low[...])
            uf, vf = u.astype(jnp.float32), v.astype(jnp.float32)
            terms = yu * (uf - vf) + yv * (uf + vf)
            part = terms[:, 0:128]
            for k in range(1, M // 128):
                part = part + terms[:, k * 128 : (k + 1) * 128]
            part = part * gain
            lanes[at] = part if f == 0 else lanes[at] + part

    slots[fr] = jnp.sum(lanes[...].T, axis=0, keepdims=True)
    for d in range(1, nf):
        c = pltpu.make_async_remote_copy(
            src_ref=slots.at[fr], dst_ref=slots.at[fr], send_sem=psend.at[d], recv_sem=precv.at[d],
            device_id=(lax.rem(fr + d, nf), me), device_id_type=MESH,
        )
        c.start()
        sends.append(c)
    for d in range(1, nf):
        ref = slots.at[lax.rem(fr + nf - d, nf)]
        pltpu.make_async_remote_copy(
            src_ref=ref, dst_ref=ref, send_sem=psend.at[d], recv_sem=precv.at[d],
            device_id=(lax.rem(fr + d, nf), me), device_id_type=MESH,
        ).wait_recv()
    power = slots[0]
    for k in range(1, nf):
        power = power + slots[k]
    power_ref[...] = power
    for c in sends:
        c.wait_send()


def on_device(snapshots, previous, replicas):
    F, _, R, M = previous.shape
    S = snapshots.shape[2]
    cells = replicas.shape[2]
    n, nf = lax.axis_size("cell"), lax.axis_size("freq")
    chips = n // 2
    T = -(-(2 * S * F + F) // 16) * 16
    dma = pltpu.SemaphoreType.DMA
    vmem = pl.BlockSpec(memory_space=pltpu.VMEM)
    power, csdm = pl.pallas_call(
        functools.partial(kernel, n, nf),
        out_shape=(
            jax.ShapeDtypeStruct((1, cells), jnp.float32),
            jax.ShapeDtypeStruct(previous.shape, jnp.float32),
        ),
        in_specs=[vmem, vmem, pl.BlockSpec(memory_space=pl.ANY)],
        out_specs=(vmem, vmem),
        scratch_shapes=[
            pltpu.VMEM((n, F, R, M), LINK),
            pltpu.VMEM((n, T, M), jnp.bfloat16),
            pltpu.VMEM(replicas.shape, jnp.bfloat16),
            pltpu.VMEM((F, M, M), jnp.float32),
            pltpu.VMEM((F, M, M), jnp.float32),
            pltpu.VMEM((M, M), jnp.bfloat16),
            pltpu.VMEM((M, M), jnp.bfloat16),
            pltpu.VMEM((cells, 128), jnp.float32),
            pltpu.VMEM((nf, 1, cells), jnp.float32),
            dma((F, chips)), dma((F, chips)), dma((F, chips)), dma((F, chips)),
            dma((chips,)), dma((chips,)), dma((chips,)), dma((chips,)),
            dma((nf,)), dma((nf,)), dma((F,)),
        ],
        compiler_params=pltpu.CompilerParams(
            collective_id=0, has_side_effects=True, vmem_limit_bytes=48 * 1024 * 1024
        ),
    )(snapshots, previous, replicas)
    return (power.reshape(cells), csdm)


def solution(mesh):
    placed = (
        P("freq", None, "cell", None),
        P("freq", None, "cell", None),
        P("freq", None, "cell", None),
    )
    return jax.shard_map(
        on_device,
        mesh=mesh,
        in_specs=placed,
        out_specs=(P("cell"), P("freq", None, "cell", None)),
        check_vma=False,
    )
```

```python
import functools

import jax
import jax.numpy as jnp
from jax import lax
from jax.experimental import pallas as pl
from jax.experimental.pallas import tpu as pltpu
from jax.sharding import PartitionSpec as P

LINK = jnp.bfloat16
LIFT = 2.0**15.5
MESH = pl.DeviceIdType.MESH


def encode(x):
    x2 = x * x
    x4 = x2 * x2
    x8 = x4 * x4
    return jnp.where(x < 0, -x8, x8).astype(LINK)


def decode(y):
    y = y.astype(jnp.float32)
    root = jnp.exp(0.125 * jnp.log(jnp.maximum(jnp.abs(y), 1e-37)))
    return jnp.where(y < 0, -root, root)


def contract_rows(a, b):
    return lax.dot_general(
        a, b, (((0,), (0,)), ((), ())), preferred_element_type=jnp.float32
    )


def dot(a, b):
    return jnp.dot(a, b, preferred_element_type=jnp.float32)


def kernel(
    n, nf, snap_ref, prev_hbm, rep_hbm, power_ref, csdm_ref,
    hbuf, mbuf, prev_ref, rep, cross_re, cross_im, weights, diag, lanes, slots,
    osend, zrecv, zsend, srecv, ssend, msend, mrecv, gsend, grecv, psend, precv, rsem, vsem,
):
    F, _, S, M = snap_ref.shape
    R = prev_ref.shape[2]
    T = mbuf.shape[1]
    cells = rep.shape[2]
    chips = n // 2
    group = 128
    per = group // R
    me = lax.axis_index("cell")
    fr = lax.axis_index("freq")
    chip, core = me // 2, lax.rem(me, 2)
    sib = chip * 2 + 1 - core

    barrier = pltpu.get_barrier_semaphore()
    for d in range(1, chips):
        pl.semaphore_signal(
            barrier, inc=1, device_id=(fr, lax.rem(chip + d, chips) * 2 + core), device_id_type=MESH
        )
    pl.semaphore_signal(barrier, inc=1, device_id=(fr, sib), device_id_type=MESH)
    for d in range(1, nf):
        pl.semaphore_signal(barrier, inc=1, device_id=(lax.rem(fr + d, nf), me), device_id_type=MESH)

    earlier = pltpu.make_async_copy(prev_hbm, prev_ref, vsem)
    earlier.start()
    loads = [pltpu.make_async_copy(rep_hbm.at[f], rep.at[f], rsem.at[f]) for f in range(F)]
    for f in range(F):
        loads[f].start()

    def ahead(d):
        return lax.rem(chip + d, chips) * 2 + core

    def behind(d):
        return lax.rem(chip + chips - d, chips) * 2 + core

    def other(d):
        return lax.rem(chip + chips - d, chips) * 2 + 1 - core

    def remote(ref, send, recv, to):
        return pltpu.make_async_remote_copy(
            src_ref=ref, dst_ref=ref, send_sem=send, recv_sem=recv,
            device_id=(fr, to), device_id_type=MESH,
        )

    earlier.wait()
    row = lax.broadcasted_iota(jnp.int32, (T, M), 0)
    message = jnp.zeros((T, M), jnp.float32)
    for f in range(F):
        for p in range(2):
            values = snap_ref[f, p].astype(jnp.float32)
            for s in range(S):
                message = jnp.where(row == (f * 2 + p) * S + s, values[s : s + 1, :], message)
        h = prev_ref[f, 0] + prev_ref[f, 1]
        top = jnp.max(jnp.max(jnp.abs(h), axis=1, keepdims=True), axis=0, keepdims=True)
        scale = jnp.maximum(top, 1e-30).astype(jnp.bfloat16).astype(jnp.float32)
        hbuf[me, f] = encode(h * (LIFT / scale))
        message = jnp.where(row == 2 * S * F + f, scale, message)
    mbuf[me] = message.astype(jnp.bfloat16)

    pl.semaphore_wait(barrier, chips - 1 + 1 + nf - 1)

    sends = []
    for d in range(chips - 1, 0, -1):
        c = remote(mbuf.at[me], msend.at[d], mrecv.at[d], ahead(d))
        c.start()
        sends.append(c)
    c = remote(mbuf.at[me], msend.at[0], mrecv.at[0], sib)
    c.start()
    sends.append(c)

    has_up, has_down = chip + 1 < chips, chip > 0
    up_to, down_to = lax.rem(me + 2, n), lax.rem(me + n - 2, n)
    for f in range(F):
        own = hbuf.at[me, f]

        @pl.when(has_up)
        def _():
            remote(own, osend.at[f, 0], zrecv.at[f, 0, 1], up_to).start()

        @pl.when(has_down)
        def _():
            remote(own, osend.at[f, 1], zrecv.at[f, 1, 1], down_to).start()

        c = remote(own, osend.at[f, 2], srecv.at[f, 1, 0], sib)
        c.start()
        sends.append(c)

    for f in range(F):
        diag[f] = jnp.zeros((1, M), jnp.float32)
        lanes[f] = jnp.zeros((cells, 128), jnp.float32)

    for d in range(1, chips):
        ref = mbuf.at[behind(d)]
        remote(ref, msend.at[d], mrecv.at[d], sib).wait_recv()
        c = remote(ref, gsend.at[d], grecv.at[d], sib)
        c.start()
        sends.append(c)
    remote(mbuf.at[sib], msend.at[0], mrecv.at[0], sib).wait_recv()
    for d in range(1, chips):
        remote(mbuf.at[other(d)], gsend.at[d], grecv.at[d], sib).wait_recv()

    factor = 0.2 / (S * n)
    G = mbuf[...].reshape(n * T, M)
    a = lax.broadcasted_iota(jnp.int32, (n * T, n * T), 0)
    b = lax.broadcasted_iota(jnp.int32, (n * T, n * T), 1)
    place = lax.rem(a, T)
    used = place < 2 * S * F
    imag = lax.rem(place, 2 * S) >= S
    turn = jnp.where(used & imag & (b == a - S), 1.0, 0.0) - jnp.where(
        used & jnp.logical_not(imag) & (b == a + S), 1.0, 0.0
    )
    Z = dot(turn.astype(jnp.bfloat16), G).astype(jnp.bfloat16)
    spot = lax.rem(lax.broadcasted_iota(jnp.int32, (n * T, M), 0), T)
    Gf = G.astype(jnp.float32)
    mine = pl.ds(pl.multiple_of(me * R, R), R)
    for f in range(F):
        inside = (spot >= 2 * S * f) & (spot < 2 * S * (f + 1))
        X = jnp.where(inside, Gf, 0.0).astype(jnp.bfloat16)
        cross_re[f] = contract_rows(X, G) * factor
        cross_im[f] = contract_rows(X, Z) * factor
        csdm_ref[f, 0] = 0.8 * prev_ref[f, 0] + cross_re[f, mine]
        csdm_ref[f, 1] = 0.8 * prev_ref[f, 1] + cross_im[f, mine]
    for f in range(F):
        loads[f].wait()

    step = min(512, cells)

    def score(g):
        for f in range(F):
            for i in range(per):
                j = g * per + i
                rows = pl.ds(pl.multiple_of(j * R, R), R)
                back = mbuf[j].astype(jnp.float32)[2 * S * F + f : 2 * S * F + f + 1, :] * (0.8 / LIFT)
                full = decode(hbuf[j, f]) * back + (cross_re[f, rows] + cross_im[f, rows])
                ii = lax.broadcasted_iota(jnp.int32, (R, M), 0)
                jj = lax.broadcasted_iota(jnp.int32, (R, M), 1)
                diag[f] += jnp.sum(jnp.where(jj == ii + j * R, full, 0.0), axis=0, keepdims=True)
                top = full.astype(jnp.bfloat16)
                weights[f, i * R : (i + 1) * R] = top
                low = (full - top.astype(jnp.float32)).astype(jnp.bfloat16)
                weights[f, group + i * R : group + (i + 1) * R] = low
            some = pl.ds(pl.multiple_of(g * group, group), group)
            for t in range(cells // step):
                at = slice(t * step, (t + 1) * step)
                us, vs = rep[f, 0, at, some], rep[f, 1, at, some]
                yu = dot(jnp.concatenate([us, us], axis=1), weights[f])
                yv = dot(jnp.concatenate([vs, vs], axis=1), weights[f])
                uf, vf = rep[f, 0, at].astype(jnp.float32), rep[f, 1, at].astype(jnp.float32)
                terms = yu * (uf - vf) + yv * (uf + vf)
                part = terms[:, 0:128]
                for k in range(1, M // 128):
                    part = part + terms[:, k * 128 : (k + 1) * 128]
                lanes[f, at] += part

    below, above = chip, chips - 1 - chip
    both = jnp.minimum(below, above)
    longer = jnp.where(below > above, 1, 0)

    def route(i):
        paired = i <= 2 * both
        k = jnp.where(paired, (i + 1) // 2, i - both)
        up = jnp.where(paired, lax.rem(i, 2), longer)
        return 1 - up, k, chip + k * (1 - 2 * up)

    def onward(f, way, k, q):
        ref = hbuf.at[q * 2 + core, f]
        later = jnp.minimum(k + 1, chips - 1)
        to = jnp.where(way == 0, up_to, down_to)
        return (
            remote(ref, zsend.at[f, way, k], zrecv.at[f, way, later], to),
            remote(ref, ssend.at[f, way, k], srecv.at[f, way, k], sib),
        )

    def goes_on(way):
        return jnp.where(way == 0, jnp.where(has_up, 1, 0), jnp.where(has_down, 1, 0)) == 1

    @pl.loop(0, chips)
    def _(i):
        way, k, q = route(i)
        for f in range(F):
            @pl.when(i > 0)
            def _():
                ref = hbuf.at[q * 2 + core, f]
                remote(ref, zsend.at[f, way, k], zrecv.at[f, way, k], sib).wait_recv()
                further, across = onward(f, way, k, q)

                @pl.when(goes_on(way))
                def _():
                    further.start()

                across.start()
        for f in range(F):
            ref = hbuf.at[q * 2 + 1 - core, f]
            remote(ref, ssend.at[f, way, k], srecv.at[f, way, k], sib).wait_recv()
        if 2 * R == group:
            score(q)

    if 2 * R != group:
        @pl.loop(0, M // group)
        def _(g):
            score(g)

    ready = jnp.zeros((cells, 128), jnp.float32)
    for f in range(F):
        ready = ready + lanes[f] * ((M / (F * nf)) / jnp.sum(diag[f], axis=1, keepdims=True))
    slots[fr] = jnp.sum(ready.T, axis=0, keepdims=True)
    for d in range(1, nf):
        c = pltpu.make_async_remote_copy(
            src_ref=slots.at[fr], dst_ref=slots.at[fr], send_sem=psend.at[d], recv_sem=precv.at[d],
            device_id=(lax.rem(fr + d, nf), me), device_id_type=MESH,
        )
        c.start()
        sends.append(c)

    for f in range(F):
        own = hbuf.at[me, f]

        @pl.when(has_up)
        def _():
            remote(own, osend.at[f, 0], zrecv.at[f, 0, 1], up_to).wait_send()

        @pl.when(has_down)
        def _():
            remote(own, osend.at[f, 1], zrecv.at[f, 1, 1], down_to).wait_send()

    @pl.loop(1, chips)
    def _(i):
        way, k, q = route(i)
        for f in range(F):
            further, across = onward(f, way, k, q)

            @pl.when(goes_on(way))
            def _():
                further.wait_send()

            across.wait_send()

    for d in range(1, nf):
        ref = slots.at[lax.rem(fr + nf - d, nf)]
        pltpu.make_async_remote_copy(
            src_ref=ref, dst_ref=ref, send_sem=psend.at[d], recv_sem=precv.at[d],
            device_id=(lax.rem(fr + d, nf), me), device_id_type=MESH,
        ).wait_recv()
    power = slots[0]
    for k in range(1, nf):
        power = power + slots[k]
    power_ref[...] = power
    for c in sends:
        c.wait_send()


def on_device(snapshots, previous, replicas):
    F, _, R, M = previous.shape
    S = snapshots.shape[2]
    cells = replicas.shape[2]
    n, nf = lax.axis_size("cell"), lax.axis_size("freq")
    chips = n // 2
    T = -(-(2 * S * F + F) // 16) * 16
    dma = pltpu.SemaphoreType.DMA
    vmem = pl.BlockSpec(memory_space=pltpu.VMEM)
    hbm = pl.BlockSpec(memory_space=pltpu.HBM)
    power, csdm = pl.pallas_call(
        functools.partial(kernel, n, nf),
        out_shape=(
            jax.ShapeDtypeStruct((1, cells), jnp.float32),
            jax.ShapeDtypeStruct(previous.shape, jnp.float32),
        ),
        in_specs=[vmem, hbm, hbm],
        out_specs=(vmem, vmem),
        scratch_shapes=[
            pltpu.VMEM((n, F, R, M), LINK),
            pltpu.VMEM((n, T, M), jnp.bfloat16),
            pltpu.VMEM(previous.shape, jnp.float32),
            pltpu.VMEM(replicas.shape, jnp.bfloat16),
            pltpu.VMEM((F, M, M), jnp.float32),
            pltpu.VMEM((F, M, M), jnp.float32),
            pltpu.VMEM((F, 256, M), jnp.bfloat16),
            pltpu.VMEM((F, 1, M), jnp.float32),
            pltpu.VMEM((F, cells, 128), jnp.float32),
            pltpu.VMEM((nf, 1, cells), jnp.float32),
            dma((F, 3)), dma((F, 2, chips)), dma((F, 2, chips)), dma((F, 2, chips)), dma((F, 2, chips)),
            dma((chips,)), dma((chips,)), dma((chips,)), dma((chips,)),
            dma((nf,)), dma((nf,)), dma((F,)), dma,
        ],
        compiler_params=pltpu.CompilerParams(
            collective_id=0, has_side_effects=True, vmem_limit_bytes=64 * 1024 * 1024 - 65536
        ),
    )(snapshots, previous, replicas)
    return (power.reshape(cells), csdm)


def solution(mesh):
    placed = (
        P("freq", None, "cell", None),
        P("freq", None, "cell", None),
        P("freq", None, "cell", None),
    )
    return jax.shard_map(
        on_device,
        mesh=mesh,
        in_specs=placed,
        out_specs=(P("cell"), P("freq", None, "cell", None)),
        check_vma=False,
    )
```

```python
import functools

import jax
import jax.numpy as jnp
from jax import lax
from jax.experimental import pallas as pl
from jax.experimental.pallas import tpu as pltpu
from jax.sharding import PartitionSpec as P

LINK = jnp.bfloat16
LIFT = 2.0**15.5
MESH = pl.DeviceIdType.MESH


def encode(x):
    x2 = x * x
    x4 = x2 * x2
    x8 = x4 * x4
    return jnp.where(x < 0, -x8, x8).astype(LINK)


def decode(y):
    y = y.astype(jnp.float32)
    root = jnp.exp(0.125 * jnp.log(jnp.maximum(jnp.abs(y), 1e-37)))
    return jnp.where(y < 0, -root, root)


def along(a, b):
    return lax.dot_general(
        a, b, (((1,), (1,)), ((), ())), preferred_element_type=jnp.float32
    )


def dot(a, b):
    return jnp.dot(a, b, preferred_element_type=jnp.float32)


def kernel(
    n, nf, snap_ref, prev_hbm, rep_hbm, power_ref, csdm_ref,
    hbuf, mbuf, prev_ref, rep, columns, weights, diag, lanes, slots,
    osend, zrecv, zsend, srecv, ssend, psend, precv, rsem, vsem,
):
    F, _, S, M = snap_ref.shape
    R = prev_ref.shape[2]
    T = mbuf.shape[1]
    cells = rep.shape[2]
    chips = n // 2
    group = 128
    per = group // R
    me = lax.axis_index("cell")
    fr = lax.axis_index("freq")
    chip, core = me // 2, lax.rem(me, 2)
    sib = chip * 2 + 1 - core

    barrier = pltpu.get_barrier_semaphore()
    for d in (2, n - 2):
        pl.semaphore_signal(barrier, inc=1, device_id=(fr, lax.rem(me + d, n)), device_id_type=MESH)
    pl.semaphore_signal(barrier, inc=1, device_id=(fr, sib), device_id_type=MESH)
    for d in range(1, nf):
        pl.semaphore_signal(barrier, inc=1, device_id=(lax.rem(fr + d, nf), me), device_id_type=MESH)

    earlier = pltpu.make_async_copy(prev_hbm, prev_ref, vsem)
    earlier.start()
    loads = [pltpu.make_async_copy(rep_hbm.at[f], rep.at[f], rsem.at[f]) for f in range(F)]
    for f in range(F):
        loads[f].start()

    def remote(ref, send, recv, to):
        return pltpu.make_async_remote_copy(
            src_ref=ref, dst_ref=ref, send_sem=send, recv_sem=recv,
            device_id=(fr, to), device_id_type=MESH,
        )

    earlier.wait()
    row = lax.broadcasted_iota(jnp.int32, (T, M), 0)
    message = jnp.zeros((T, M), jnp.float32)
    for f in range(F):
        for p in range(2):
            values = snap_ref[f, p].astype(jnp.float32)
            for s in range(S):
                message = jnp.where(row == (f * 2 + p) * S + s, values[s : s + 1, :], message)
        h = prev_ref[f, 0] + prev_ref[f, 1]
        top = jnp.max(jnp.max(jnp.abs(h), axis=1, keepdims=True), axis=0, keepdims=True)
        scale = jnp.maximum(top, 1e-30).astype(jnp.bfloat16).astype(jnp.float32)
        hbuf[me, f] = encode(h * (LIFT / scale))
        message = jnp.where(row == 2 * S * F + f, scale, message)
    mbuf[me] = message.astype(jnp.bfloat16)

    pl.semaphore_wait(barrier, 2 + 1 + nf - 1)

    sends = []
    has_up, has_down = chip + 1 < chips, chip > 0
    up_to, down_to = lax.rem(me + 2, n), lax.rem(me + n - 2, n)
    def piece(x, c):
        return mbuf.at[c] if x == 0 else hbuf.at[c, x - 1]

    for x in range(F + 1):
        own = piece(x, me)

        @pl.when(has_up)
        def _():
            remote(own, osend.at[x, 0], zrecv.at[x, 0, 1], up_to).start()

        @pl.when(has_down)
        def _():
            remote(own, osend.at[x, 1], zrecv.at[x, 1, 1], down_to).start()

        c = remote(own, osend.at[x, 2], srecv.at[x, 1, 0], sib)
        c.start()
        sends.append(c)

    for f in range(F):
        diag[f] = jnp.zeros((1, M), jnp.float32)
        lanes[f] = jnp.zeros((cells, 128), jnp.float32)
    for f in range(F):
        loads[f].wait()

    step = min(512, cells)

    def score(g, f):
        for i in range(per):
            j = g * per + i
            back = mbuf[j].astype(jnp.float32)[2 * S * F + f : 2 * S * F + f + 1, :] * (0.8 / LIFT)
            full = decode(hbuf[j, f]) * back
            ii = lax.broadcasted_iota(jnp.int32, (R, M), 0)
            jj = lax.broadcasted_iota(jnp.int32, (R, M), 1)
            diag[f] += jnp.sum(jnp.where(jj == ii + j * R, full, 0.0), axis=0, keepdims=True)
            top = full.astype(jnp.bfloat16)
            weights[f, i * R : (i + 1) * R] = top
            low = (full - top.astype(jnp.float32)).astype(jnp.bfloat16)
            weights[f, group + i * R : group + (i + 1) * R] = low
        some = pl.ds(pl.multiple_of(g * group, group), group)
        for t in range(cells // step):
            at = slice(t * step, (t + 1) * step)
            us, vs = rep[f, 0, at, some], rep[f, 1, at, some]
            yu = dot(jnp.concatenate([us, us], axis=1), weights[f])
            yv = dot(jnp.concatenate([vs, vs], axis=1), weights[f])
            uf, vf = rep[f, 0, at].astype(jnp.float32), rep[f, 1, at].astype(jnp.float32)
            terms = yu * (uf - vf) + yv * (uf + vf)
            part = terms[:, 0:128]
            for k in range(1, M // 128):
                part = part + terms[:, k * 128 : (k + 1) * 128]
            lanes[f, at] += part

    below, above = chip, chips - 1 - chip
    both = jnp.minimum(below, above)
    longer = jnp.where(below > above, 1, 0)

    def route(i):
        paired = i <= 2 * both
        k = jnp.where(paired, (i + 1) // 2, i - both)
        up = jnp.where(paired, lax.rem(i, 2), longer)
        return 1 - up, k, chip + k * (1 - 2 * up)

    def onward(x, way, k):
        q = chip - k if way == 0 else chip + k
        ref = piece(x, q * 2 + core)
        to = up_to if way == 0 else down_to
        later = jnp.minimum(k + 1, chips - 1)
        return (
            remote(ref, zsend.at[x, way, k], zrecv.at[x, way, k], sib),
            remote(ref, zsend.at[x, way, k], zrecv.at[x, way, later], to),
            remote(ref, ssend.at[x, way, k], srecv.at[x, way, k], sib),
        )

    goes_on = (has_up, has_down)

    def pass_on(k):
        for way in range(2):
            @pl.when((k <= below) if way == 0 else (k <= above))
            def _():
                for x in range(F + 1):
                    arrival, further, across = onward(x, way, k)
                    arrival.wait_recv()

                    @pl.when(goes_on[way])
                    def _():
                        further.start()

                    across.start()

    @pl.loop(0, chips)
    def _(i):
        way, k, q = route(i)
        for x in range(F + 1):
            ref = piece(x, q * 2 + 1 - core)
            remote(ref, ssend.at[x, way, k], srecv.at[x, way, k], sib).wait_recv()
        if 2 * R == group:
            score(q, 0)
        pass_on(i + 1)
        if 2 * R == group:
            for f in range(1, F):
                score(q, f)

    if 2 * R != group:
        @pl.loop(0, M // group)
        def _(g):
            for f in range(F):
                score(g, f)

    factor = 0.2 / (S * n)
    G = mbuf[...].reshape(n * T, M)
    a = lax.broadcasted_iota(jnp.int32, (n * T, n * T), 0)
    b = lax.broadcasted_iota(jnp.int32, (n * T, n * T), 1)
    place = lax.rem(a, T)
    used = place < 2 * S * F
    imag = lax.rem(place, 2 * S) >= S
    turn = jnp.where(used & imag & (b == a - S), 1.0, 0.0) - jnp.where(
        used & jnp.logical_not(imag) & (b == a + S), 1.0, 0.0
    )
    Zf = dot(turn.astype(jnp.bfloat16), G)
    Z = Zf.astype(jnp.bfloat16)
    spot = lax.rem(lax.broadcasted_iota(jnp.int32, (n * T, M), 0), T)
    Gf = G.astype(jnp.float32)
    ready = jnp.zeros((cells, 128), jnp.float32)
    columns[...] = Gf.T
    mine = columns[pl.ds(pl.multiple_of(me * R, R), R), :]
    lane = lax.rem(lax.broadcasted_iota(jnp.int32, (R, n * T), 1), T)
    for f in range(F):
        first, last = 2 * S * f, 2 * S * (f + 1)
        left = jnp.where((lane >= first) & (lane < last), mine, 0.0).astype(jnp.bfloat16)
        csdm_ref[f, 0] = 0.8 * prev_ref[f, 0] + factor * dot(left, G)
        csdm_ref[f, 1] = 0.8 * prev_ref[f, 1] + factor * dot(left, Z)
        inside = (spot >= first) & (spot < last)
        X = jnp.where(inside, Gf, 0.0)
        field = along(rep[f, 0], X.astype(jnp.bfloat16)) - along(
            rep[f, 1], jnp.where(inside, Zf, 0.0).astype(jnp.bfloat16)
        )
        squares = field * field
        part = squares[:, 0:128]
        for k in range(1, n * T // 128):
            part = part + squares[:, k * 128 : (k + 1) * 128]
        every = diag[f] + factor * jnp.sum(X * X, axis=0, keepdims=True)
        gain = (M / (F * nf)) / jnp.sum(every, axis=1, keepdims=True)
        ready = ready + (lanes[f] + factor * part) * gain
    slots[fr] = jnp.sum(ready.T, axis=0, keepdims=True)
    for d in range(1, nf):
        c = pltpu.make_async_remote_copy(
            src_ref=slots.at[fr], dst_ref=slots.at[fr], send_sem=psend.at[d], recv_sem=precv.at[d],
            device_id=(lax.rem(fr + d, nf), me), device_id_type=MESH,
        )
        c.start()
        sends.append(c)

    for x in range(F + 1):
        own = piece(x, me)

        @pl.when(has_up)
        def _():
            remote(own, osend.at[x, 0], zrecv.at[x, 0, 1], up_to).wait_send()

        @pl.when(has_down)
        def _():
            remote(own, osend.at[x, 1], zrecv.at[x, 1, 1], down_to).wait_send()

    @pl.loop(1, chips)
    def _(k):
        for way in range(2):
            @pl.when((k <= below) if way == 0 else (k <= above))
            def _():
                for x in range(F + 1):
                    _, further, across = onward(x, way, k)

                    @pl.when(goes_on[way])
                    def _():
                        further.wait_send()

                    across.wait_send()

    for d in range(1, nf):
        ref = slots.at[lax.rem(fr + nf - d, nf)]
        pltpu.make_async_remote_copy(
            src_ref=ref, dst_ref=ref, send_sem=psend.at[d], recv_sem=precv.at[d],
            device_id=(lax.rem(fr + d, nf), me), device_id_type=MESH,
        ).wait_recv()
    power = slots[0]
    for k in range(1, nf):
        power = power + slots[k]
    power_ref[...] = power
    for c in sends:
        c.wait_send()


def on_device(snapshots, previous, replicas):
    F, _, R, M = previous.shape
    S = snapshots.shape[2]
    cells = replicas.shape[2]
    n, nf = lax.axis_size("cell"), lax.axis_size("freq")
    chips = n // 2
    T = -(-(2 * S * F + F) // 16) * 16
    dma = pltpu.SemaphoreType.DMA
    vmem = pl.BlockSpec(memory_space=pltpu.VMEM)
    hbm = pl.BlockSpec(memory_space=pltpu.HBM)
    power, csdm = pl.pallas_call(
        functools.partial(kernel, n, nf),
        out_shape=(
            jax.ShapeDtypeStruct((1, cells), jnp.float32),
            jax.ShapeDtypeStruct(previous.shape, jnp.float32),
        ),
        in_specs=[vmem, hbm, hbm],
        out_specs=(vmem, vmem),
        scratch_shapes=[
            pltpu.VMEM((n, F, R, M), LINK),
            pltpu.VMEM((n, T, M), jnp.bfloat16),
            pltpu.VMEM(previous.shape, jnp.float32),
            pltpu.VMEM(replicas.shape, jnp.bfloat16),
            pltpu.VMEM((M, n * T), jnp.float32),
            pltpu.VMEM((F, 256, M), jnp.bfloat16),
            pltpu.VMEM((F, 1, M), jnp.float32),
            pltpu.VMEM((F, cells, 128), jnp.float32),
            pltpu.VMEM((nf, 1, cells), jnp.float32),
            dma((F + 1, 3)), dma((F + 1, 2, chips)), dma((F + 1, 2, chips)),
            dma((F + 1, 2, chips)), dma((F + 1, 2, chips)),
            dma((nf,)), dma((nf,)), dma((F,)), dma,
        ],
        compiler_params=pltpu.CompilerParams(
            collective_id=0, has_side_effects=True, vmem_limit_bytes=64 * 1024 * 1024 - 65536
        ),
    )(snapshots, previous, replicas)
    return (power.reshape(cells), csdm)


def solution(mesh):
    placed = (
        P("freq", None, "cell", None),
        P("freq", None, "cell", None),
        P("freq", None, "cell", None),
    )
    return jax.shard_map(
        on_device,
        mesh=mesh,
        in_specs=placed,
        out_specs=(P("cell"), P("freq", None, "cell", None)),
        check_vma=False,
    )
```

```python
import functools

import jax
import jax.numpy as jnp
from jax import lax
from jax.experimental import pallas as pl
from jax.experimental.pallas import tpu as pltpu
from jax.sharding import PartitionSpec as P

LINK = jnp.bfloat16
LIFT = 2.0**15.5
MESH = pl.DeviceIdType.MESH


def encode(x):
    x2 = x * x
    x4 = x2 * x2
    x8 = x4 * x4
    return jnp.where(x < 0, -x8, x8).astype(LINK)


def decode(y):
    y = y.astype(jnp.float32)
    root = jnp.exp(0.125 * jnp.log(jnp.maximum(jnp.abs(y), 1e-37)))
    return jnp.where(y < 0, -root, root)


def along(a, b):
    return lax.dot_general(
        a, b, (((1,), (1,)), ((), ())), preferred_element_type=jnp.float32
    )


def dot(a, b):
    return jnp.dot(a, b, preferred_element_type=jnp.float32)


def kernel(
    n, nf, snap_ref, prev_hbm, rep_hbm, power_ref, csdm_ref,
    hbuf, mbuf, prev_ref, rep, columns, weights, diag, lanes, slots,
    osend, zrecv, zsend, srecv, ssend, psend, precv, rsem, vsem,
):
    F, _, S, M = snap_ref.shape
    R = prev_ref.shape[2]
    T = mbuf.shape[1]
    cells = rep.shape[2]
    chips = n // 2
    group = 128
    per = group // R
    me = lax.axis_index("cell")
    fr = lax.axis_index("freq")
    chip, core = me // 2, lax.rem(me, 2)
    sib = chip * 2 + 1 - core

    barrier = pltpu.get_barrier_semaphore()
    for d in (2, n - 2):
        pl.semaphore_signal(barrier, inc=1, device_id=(fr, lax.rem(me + d, n)), device_id_type=MESH)
    pl.semaphore_signal(barrier, inc=1, device_id=(fr, sib), device_id_type=MESH)
    for d in range(1, nf):
        pl.semaphore_signal(barrier, inc=1, device_id=(lax.rem(fr + d, nf), me), device_id_type=MESH)

    earlier = pltpu.make_async_copy(prev_hbm, prev_ref, vsem)
    earlier.start()
    loads = [pltpu.make_async_copy(rep_hbm.at[f], rep.at[f], rsem.at[f]) for f in range(F)]
    for f in range(F):
        loads[f].start()

    def remote(ref, send, recv, to):
        return pltpu.make_async_remote_copy(
            src_ref=ref, dst_ref=ref, send_sem=send, recv_sem=recv,
            device_id=(fr, to), device_id_type=MESH,
        )

    earlier.wait()
    row = lax.broadcasted_iota(jnp.int32, (T, M), 0)
    message = jnp.zeros((T, M), jnp.float32)
    for f in range(F):
        for p in range(2):
            values = snap_ref[f, p].astype(jnp.float32)
            for s in range(S):
                message = jnp.where(row == (f * 2 + p) * S + s, values[s : s + 1, :], message)
        h = prev_ref[f, 0] + prev_ref[f, 1]
        top = jnp.max(jnp.max(jnp.abs(h), axis=1, keepdims=True), axis=0, keepdims=True)
        scale = jnp.maximum(top, 1e-30).astype(jnp.bfloat16).astype(jnp.float32)
        hbuf[me, f] = encode(h * (LIFT / scale))
        message = jnp.where(row == 2 * S * F + f, scale, message)
    mbuf[me] = message.astype(jnp.bfloat16)

    pl.semaphore_wait(barrier, 2 + 1 + nf - 1)

    sends = []
    has_up, has_down = chip + 1 < chips, chip > 0
    up_to, down_to = lax.rem(me + 2, n), lax.rem(me + n - 2, n)
    def piece(x, c):
        return mbuf.at[c] if x == 0 else hbuf.at[c, x - 1]

    for x in range(F + 1):
        own = piece(x, me)

        @pl.when(has_up)
        def _():
            remote(own, osend.at[x, 0], zrecv.at[x, 0, 1], up_to).start()

        @pl.when(has_down)
        def _():
            remote(own, osend.at[x, 1], zrecv.at[x, 1, 1], down_to).start()

        c = remote(own, osend.at[x, 2], srecv.at[x, 1, 0], sib)
        c.start()
        sends.append(c)

    for f in range(F):
        diag[f] = jnp.zeros((1, M), jnp.float32)
        lanes[f] = jnp.zeros((cells, 128), jnp.float32)
    for f in range(F):
        loads[f].wait()

    step = min(512, cells)

    def score(g, f):
        for i in range(per):
            j = g * per + i
            back = mbuf[j].astype(jnp.float32)[2 * S * F + f : 2 * S * F + f + 1, :] * (0.8 / LIFT)
            full = decode(hbuf[j, f]) * back
            ii = lax.broadcasted_iota(jnp.int32, (R, M), 0)
            jj = lax.broadcasted_iota(jnp.int32, (R, M), 1)
            diag[f] += jnp.sum(jnp.where(jj == ii + j * R, full, 0.0), axis=0, keepdims=True)
            top = full.astype(jnp.bfloat16)
            weights[f, i * R : (i + 1) * R] = top
            low = (full - top.astype(jnp.float32)).astype(jnp.bfloat16)
            weights[f, group + i * R : group + (i + 1) * R] = low
        some = pl.ds(pl.multiple_of(g * group, group), group)
        for t in range(cells // step):
            at = slice(t * step, (t + 1) * step)
            us, vs = rep[f, 0, at, some], rep[f, 1, at, some]
            yu = dot(jnp.concatenate([us, us], axis=1), weights[f])
            yv = dot(jnp.concatenate([vs, vs], axis=1), weights[f])
            uf, vf = rep[f, 0, at].astype(jnp.float32), rep[f, 1, at].astype(jnp.float32)
            terms = yu * (uf - vf) + yv * (uf + vf)
            part = terms[:, 0:128]
            for k in range(1, M // 128):
                part = part + terms[:, k * 128 : (k + 1) * 128]
            lanes[f, at] += part

    below, above = chip, chips - 1 - chip
    both = jnp.minimum(below, above)
    longer = jnp.where(below > above, 1, 0)

    def route(i):
        paired = i <= 2 * both
        k = jnp.where(paired, (i + 1) // 2, i - both)
        up = jnp.where(paired, lax.rem(i, 2), longer)
        return 1 - up, k, chip + k * (1 - 2 * up)

    def onward(x, way, k):
        q = chip - k if way == 0 else chip + k
        ref = piece(x, q * 2 + core)
        to = up_to if way == 0 else down_to
        later = jnp.minimum(k + 1, chips - 1)
        return (
            remote(ref, zsend.at[x, way, k], zrecv.at[x, way, k], sib),
            remote(ref, zsend.at[x, way, k], zrecv.at[x, way, later], to),
            remote(ref, ssend.at[x, way, k], srecv.at[x, way, k], sib),
        )

    goes_on = (has_up, has_down)

    def pass_on(k):
        for way in range(2):
            @pl.when((k <= below) if way == 0 else (k <= above))
            def _():
                for x in range(F + 1):
                    arrival, further, across = onward(x, way, k)
                    arrival.wait_recv()

                    @pl.when(goes_on[way])
                    def _():
                        further.start()

                    across.start()

    @pl.loop(0, chips)
    def _(i):
        way, k, q = route(i)
        for x in range(F + 1):
            ref = piece(x, q * 2 + 1 - core)
            remote(ref, ssend.at[x, way, k], srecv.at[x, way, k], sib).wait_recv()
        if 2 * R == group:
            score(q, 0)
        pass_on(i + 1)
        if 2 * R == group:
            for f in range(1, F):
                score(q, f)

    if 2 * R != group:
        @pl.loop(0, M // group)
        def _(g):
            for f in range(F):
                score(g, f)

    factor = 0.2 / (S * n)
    G = mbuf[...].reshape(n * T, M)
    a = lax.broadcasted_iota(jnp.int32, (n * T, n * T), 0)
    b = lax.broadcasted_iota(jnp.int32, (n * T, n * T), 1)
    place = lax.rem(a, T)
    used = place < 2 * S * F
    imag = lax.rem(place, 2 * S) >= S
    turn = jnp.where(used & imag & (b == a - S), 1.0, 0.0) - jnp.where(
        used & jnp.logical_not(imag) & (b == a + S), 1.0, 0.0
    )
    Zf = dot(turn.astype(jnp.bfloat16), G)
    Z = Zf.astype(jnp.bfloat16)
    spot = lax.rem(lax.broadcasted_iota(jnp.int32, (n * T, M), 0), T)
    Gf = G.astype(jnp.float32)
    ready = jnp.zeros((cells, 128), jnp.float32)
    columns[...] = Gf.T
    mine = columns[pl.ds(pl.multiple_of(me * R, R), R), :]
    lane = lax.rem(lax.broadcasted_iota(jnp.int32, (R, n * T), 1), T)
    for f in range(F):
        first, last = 2 * S * f, 2 * S * (f + 1)
        left = jnp.where((lane >= first) & (lane < last), mine, 0.0).astype(jnp.bfloat16)
        csdm_ref[f, 0] = 0.8 * prev_ref[f, 0] + factor * dot(left, G)
        csdm_ref[f, 1] = 0.8 * prev_ref[f, 1] + factor * dot(left, Z)
        inside = (spot >= first) & (spot < last)
        X = jnp.where(inside, Gf, 0.0)
        field = along(rep[f, 0], X.astype(jnp.bfloat16)) - along(
            rep[f, 1], jnp.where(inside, Zf, 0.0).astype(jnp.bfloat16)
        )
        squares = field * field
        part = squares[:, 0:128]
        for k in range(1, n * T // 128):
            part = part + squares[:, k * 128 : (k + 1) * 128]
        every = diag[f] + factor * jnp.sum(X * X, axis=0, keepdims=True)
        gain = (M / (F * nf)) / jnp.sum(every, axis=1, keepdims=True)
        ready = ready + (lanes[f] + factor * part) * gain
    slots[fr] = jnp.sum(ready.T, axis=0, keepdims=True)
    for d in range(1, nf):
        c = pltpu.make_async_remote_copy(
            src_ref=slots.at[fr], dst_ref=slots.at[fr], send_sem=psend.at[d], recv_sem=precv.at[d],
            device_id=(lax.rem(fr + d, nf), me), device_id_type=MESH,
        )
        c.start()
        sends.append(c)

    for x in range(F + 1):
        own = piece(x, me)

        @pl.when(has_up)
        def _():
            remote(own, osend.at[x, 0], zrecv.at[x, 0, 1], up_to).wait_send()

        @pl.when(has_down)
        def _():
            remote(own, osend.at[x, 1], zrecv.at[x, 1, 1], down_to).wait_send()

    @pl.loop(1, chips)
    def _(k):
        for way in range(2):
            @pl.when((k <= below) if way == 0 else (k <= above))
            def _():
                for x in range(F + 1):
                    _, further, across = onward(x, way, k)

                    @pl.when(goes_on[way])
                    def _():
                        further.wait_send()

                    across.wait_send()

    for d in range(1, nf):
        ref = slots.at[lax.rem(fr + nf - d, nf)]
        pltpu.make_async_remote_copy(
            src_ref=ref, dst_ref=ref, send_sem=psend.at[d], recv_sem=precv.at[d],
            device_id=(lax.rem(fr + d, nf), me), device_id_type=MESH,
        ).wait_recv()
    power = slots[0]
    for k in range(1, nf):
        power = power + slots[k]
    power_ref[...] = power
    for c in sends:
        c.wait_send()


def on_device(snapshots, previous, replicas):
    F, _, R, M = previous.shape
    S = snapshots.shape[2]
    cells = replicas.shape[2]
    n, nf = lax.axis_size("cell"), lax.axis_size("freq")
    chips = n // 2
    T = -(-(2 * S * F + F) // 16) * 16
    dma = pltpu.SemaphoreType.DMA
    vmem = pl.BlockSpec(memory_space=pltpu.VMEM)
    hbm = pl.BlockSpec(memory_space=pltpu.HBM)
    power, csdm = pl.pallas_call(
        functools.partial(kernel, n, nf),
        out_shape=(
            jax.ShapeDtypeStruct((1, cells), jnp.float32),
            jax.ShapeDtypeStruct(previous.shape, jnp.float32),
        ),
        in_specs=[vmem, hbm, hbm],
        out_specs=(vmem, vmem),
        scratch_shapes=[
            pltpu.VMEM((n, F, R, M), LINK),
            pltpu.VMEM((n, T, M), jnp.bfloat16),
            pltpu.VMEM(previous.shape, jnp.float32),
            pltpu.VMEM(replicas.shape, jnp.bfloat16),
            pltpu.VMEM((M, n * T), jnp.float32),
            pltpu.VMEM((F, 256, M), jnp.bfloat16),
            pltpu.VMEM((F, 1, M), jnp.float32),
            pltpu.VMEM((F, cells, 128), jnp.float32),
            pltpu.VMEM((nf, 1, cells), jnp.float32),
            dma((F + 1, 3)), dma((F + 1, 2, chips)), dma((F + 1, 2, chips)),
            dma((F + 1, 2, chips)), dma((F + 1, 2, chips)),
            dma((nf,)), dma((nf,)), dma((F,)), dma,
        ],
        compiler_params=pltpu.CompilerParams(
            collective_id=0, has_side_effects=True, vmem_limit_bytes=48 * 1024 * 1024
        ),
    )(snapshots, pltpu.with_memory_space_constraint(previous, pltpu.HBM), pltpu.with_memory_space_constraint(replicas, pltpu.HBM))
    return (power.reshape(cells), csdm)


def solution(mesh):
    placed = (
        P("freq", None, "cell", None),
        P("freq", None, "cell", None),
        P("freq", None, "cell", None),
    )
    return jax.shard_map(
        on_device,
        mesh=mesh,
        in_specs=placed,
        out_specs=(P("cell"), P("freq", None, "cell", None)),
        check_vma=False,
    )
```

```python
import functools

import jax
import jax.numpy as jnp
from jax import lax
from jax.experimental import pallas as pl
from jax.experimental.pallas import tpu as pltpu
from jax.sharding import PartitionSpec as P

LINK = jnp.bfloat16
LIFT = 2.0**15.5
MESH = pl.DeviceIdType.MESH


def encode(x):
    x2 = x * x
    x4 = x2 * x2
    x8 = x4 * x4
    return jnp.where(x < 0, -x8, x8).astype(LINK)


def decode(y):
    y = y.astype(jnp.float32)
    root = jnp.exp(0.125 * jnp.log(jnp.maximum(jnp.abs(y), 1e-37)))
    return jnp.where(y < 0, -root, root)


def along(a, b):
    return lax.dot_general(
        a, b, (((1,), (1,)), ((), ())), preferred_element_type=jnp.float32
    )


def dot(a, b):
    return jnp.dot(a, b, preferred_element_type=jnp.float32)


def kernel(
    n, nf, snap_ref, prev_hbm, rep_hbm, power_ref, csdm_ref,
    hbuf, mbuf, prev_ref, rep, columns, weights, diag, lanes, slots,
    osend, zrecv, zsend, srecv, ssend, psend, precv, rsem, vsem,
):
    F, _, S, M = snap_ref.shape
    R = prev_ref.shape[2]
    T = mbuf.shape[1]
    cells = rep.shape[2]
    chips = n // 2
    group = 128
    per = group // R
    me = lax.axis_index("cell")
    fr = lax.axis_index("freq")
    chip, core = me // 2, lax.rem(me, 2)
    sib = chip * 2 + 1 - core

    barrier = pltpu.get_barrier_semaphore()
    for d in (2, n - 2):
        pl.semaphore_signal(barrier, inc=1, device_id=(fr, lax.rem(me + d, n)), device_id_type=MESH)
    pl.semaphore_signal(barrier, inc=1, device_id=(fr, sib), device_id_type=MESH)
    for d in range(1, nf):
        pl.semaphore_signal(barrier, inc=1, device_id=(lax.rem(fr + d, nf), me), device_id_type=MESH)

    earlier = pltpu.make_async_copy(prev_hbm, prev_ref, vsem)
    earlier.start()
    loads = [pltpu.make_async_copy(rep_hbm.at[f], rep.at[f], rsem.at[f]) for f in range(F)]
    for f in range(F):
        loads[f].start()

    def remote(ref, send, recv, to):
        return pltpu.make_async_remote_copy(
            src_ref=ref, dst_ref=ref, send_sem=send, recv_sem=recv,
            device_id=(fr, to), device_id_type=MESH,
        )

    earlier.wait()
    row = lax.broadcasted_iota(jnp.int32, (T, M), 0)
    message = jnp.zeros((T, M), jnp.float32)
    for f in range(F):
        for p in range(2):
            values = snap_ref[f, p].astype(jnp.float32)
            for s in range(S):
                message = jnp.where(row == (f * 2 + p) * S + s, values[s : s + 1, :], message)
        h = prev_ref[f, 0] + prev_ref[f, 1]
        top = jnp.max(jnp.max(jnp.abs(h), axis=1, keepdims=True), axis=0, keepdims=True)
        scale = jnp.maximum(top, 1e-30).astype(jnp.bfloat16).astype(jnp.float32)
        hbuf[me, f] = encode(h * (LIFT / scale))
        message = jnp.where(row == 2 * S * F + f, scale, message)
    mbuf[me] = message.astype(jnp.bfloat16)

    pl.semaphore_wait(barrier, 2 + 1 + nf - 1)

    sends = []
    has_up, has_down = chip + 1 < chips, chip > 0
    up_to, down_to = lax.rem(me + 2, n), lax.rem(me + n - 2, n)
    def piece(x, c):
        return mbuf.at[c] if x == 0 else hbuf.at[c, x - 1]

    for x in range(F + 1):
        own = piece(x, me)

        @pl.when(has_up)
        def _():
            remote(own, osend.at[x, 0], zrecv.at[x, 0, 1], up_to).start()

        @pl.when(has_down)
        def _():
            remote(own, osend.at[x, 1], zrecv.at[x, 1, 1], down_to).start()

        c = remote(own, osend.at[x, 2], srecv.at[x, 1, 0], sib)
        c.start()
        sends.append(c)

    for f in range(F):
        diag[f] = jnp.zeros((1, M), jnp.float32)
        lanes[f] = jnp.zeros((cells, 128), jnp.float32)
    for f in range(F):
        loads[f].wait()

    step = min(512, cells)

    def score(g, f):
        for i in range(per):
            j = g * per + i
            back = mbuf[j].astype(jnp.float32)[2 * S * F + f : 2 * S * F + f + 1, :] * (0.8 / LIFT)
            full = decode(hbuf[j, f]) * back
            ii = lax.broadcasted_iota(jnp.int32, (R, M), 0)
            jj = lax.broadcasted_iota(jnp.int32, (R, M), 1)
            diag[f] += jnp.sum(jnp.where(jj == ii + j * R, full, 0.0), axis=0, keepdims=True)
            top = full.astype(jnp.bfloat16)
            weights[f, i * R : (i + 1) * R] = top
            low = (full - top.astype(jnp.float32)).astype(jnp.bfloat16)
            weights[f, group + i * R : group + (i + 1) * R] = low
        some = pl.ds(pl.multiple_of(g * group, group), group)
        for t in range(cells // step):
            at = slice(t * step, (t + 1) * step)
            us, vs = rep[f, 0, at, some], rep[f, 1, at, some]
            yu = dot(jnp.concatenate([us, us], axis=1), weights[f])
            yv = dot(jnp.concatenate([vs, vs], axis=1), weights[f])
            uf, vf = rep[f, 0, at].astype(jnp.float32), rep[f, 1, at].astype(jnp.float32)
            terms = yu * (uf - vf) + yv * (uf + vf)
            part = terms[:, 0:128]
            for k in range(1, M // 128):
                part = part + terms[:, k * 128 : (k + 1) * 128]
            lanes[f, at] += part

    below, above = chip, chips - 1 - chip
    both = jnp.minimum(below, above)
    longer = jnp.where(below > above, 1, 0)

    def route(i):
        paired = i <= 2 * both
        k = jnp.where(paired, (i + 1) // 2, i - both)
        up = jnp.where(paired, lax.rem(i, 2), longer)
        return 1 - up, k, chip + k * (1 - 2 * up)

    def onward(x, way, k):
        q = chip - k if way == 0 else chip + k
        ref = piece(x, q * 2 + core)
        to = up_to if way == 0 else down_to
        later = jnp.minimum(k + 1, chips - 1)
        return (
            remote(ref, zsend.at[x, way, k], zrecv.at[x, way, k], sib),
            remote(ref, zsend.at[x, way, k], zrecv.at[x, way, later], to),
            remote(ref, ssend.at[x, way, k], srecv.at[x, way, k], sib),
        )

    goes_on = (has_up, has_down)

    def pass_on(k):
        for way in range(2):
            @pl.when((k <= below) if way == 0 else (k <= above))
            def _():
                for x in range(F + 1):
                    arrival, further, across = onward(x, way, k)
                    arrival.wait_recv()

                    @pl.when(goes_on[way])
                    def _():
                        further.start()

                    across.start()

    @pl.loop(0, chips)
    def _(i):
        way, k, q = route(i)
        for x in range(F + 1):
            ref = piece(x, q * 2 + 1 - core)
            remote(ref, ssend.at[x, way, k], srecv.at[x, way, k], sib).wait_recv()
        if 2 * R == group:
            score(q, 0)
        pass_on(i + 1)
        if 2 * R == group:
            for f in range(1, F):
                score(q, f)

    if 2 * R != group:
        @pl.loop(0, M // group)
        def _(g):
            for f in range(F):
                score(g, f)

    factor = 0.2 / (S * n)
    G = mbuf[...].reshape(n * T, M)
    a = lax.broadcasted_iota(jnp.int32, (n * T, n * T), 0)
    b = lax.broadcasted_iota(jnp.int32, (n * T, n * T), 1)
    place = lax.rem(a, T)
    used = place < 2 * S * F
    imag = lax.rem(place, 2 * S) >= S
    turn = jnp.where(used & imag & (b == a - S), 1.0, 0.0) - jnp.where(
        used & jnp.logical_not(imag) & (b == a + S), 1.0, 0.0
    )
    Zf = dot(turn.astype(jnp.bfloat16), G)
    Z = Zf.astype(jnp.bfloat16)
    spot = lax.rem(lax.broadcasted_iota(jnp.int32, (n * T, M), 0), T)
    Gf = G.astype(jnp.float32)
    ready = jnp.zeros((cells, 128), jnp.float32)
    for f in range(F):
        first, last = 2 * S * f, 2 * S * (f + 1)
        inside = (spot >= first) & (spot < last)
        X = jnp.where(inside, Gf, 0.0)
        field = along(rep[f, 0], X.astype(jnp.bfloat16)) - along(
            rep[f, 1], jnp.where(inside, Zf, 0.0).astype(jnp.bfloat16)
        )
        squares = field * field
        part = squares[:, 0:128]
        for k in range(1, n * T // 128):
            part = part + squares[:, k * 128 : (k + 1) * 128]
        every = diag[f] + factor * jnp.sum(X * X, axis=0, keepdims=True)
        gain = (M / (F * nf)) / jnp.sum(every, axis=1, keepdims=True)
        ready = ready + (lanes[f] + factor * part) * gain
    slots[fr] = jnp.sum(ready.T, axis=0, keepdims=True)
    for d in range(1, nf):
        c = pltpu.make_async_remote_copy(
            src_ref=slots.at[fr], dst_ref=slots.at[fr], send_sem=psend.at[d], recv_sem=precv.at[d],
            device_id=(lax.rem(fr + d, nf), me), device_id_type=MESH,
        )
        c.start()
        sends.append(c)

    columns[...] = Gf.T
    mine = columns[pl.ds(pl.multiple_of(me * R, R), R), :]
    lane = lax.rem(lax.broadcasted_iota(jnp.int32, (R, n * T), 1), T)
    for f in range(F):
        first, last = 2 * S * f, 2 * S * (f + 1)
        left = jnp.where((lane >= first) & (lane < last), mine, 0.0).astype(jnp.bfloat16)
        csdm_ref[f, 0] = 0.8 * prev_ref[f, 0] + factor * dot(left, G)
        csdm_ref[f, 1] = 0.8 * prev_ref[f, 1] + factor * dot(left, Z)

    for x in range(F + 1):
        own = piece(x, me)

        @pl.when(has_up)
        def _():
            remote(own, osend.at[x, 0], zrecv.at[x, 0, 1], up_to).wait_send()

        @pl.when(has_down)
        def _():
            remote(own, osend.at[x, 1], zrecv.at[x, 1, 1], down_to).wait_send()

    @pl.loop(1, chips)
    def _(k):
        for way in range(2):
            @pl.when((k <= below) if way == 0 else (k <= above))
            def _():
                for x in range(F + 1):
                    _, further, across = onward(x, way, k)

                    @pl.when(goes_on[way])
                    def _():
                        further.wait_send()

                    across.wait_send()

    for d in range(1, nf):
        ref = slots.at[lax.rem(fr + nf - d, nf)]
        pltpu.make_async_remote_copy(
            src_ref=ref, dst_ref=ref, send_sem=psend.at[d], recv_sem=precv.at[d],
            device_id=(lax.rem(fr + d, nf), me), device_id_type=MESH,
        ).wait_recv()
    power = slots[0]
    for k in range(1, nf):
        power = power + slots[k]
    power_ref[...] = power
    for c in sends:
        c.wait_send()


def on_device(snapshots, previous, replicas):
    F, _, R, M = previous.shape
    S = snapshots.shape[2]
    cells = replicas.shape[2]
    n, nf = lax.axis_size("cell"), lax.axis_size("freq")
    chips = n // 2
    T = -(-(2 * S * F + F) // 16) * 16
    dma = pltpu.SemaphoreType.DMA
    vmem = pl.BlockSpec(memory_space=pltpu.VMEM)
    hbm = pl.BlockSpec(memory_space=pltpu.HBM)
    power, csdm = pl.pallas_call(
        functools.partial(kernel, n, nf),
        out_shape=(
            jax.ShapeDtypeStruct((1, cells), jnp.float32),
            jax.ShapeDtypeStruct(previous.shape, jnp.float32),
        ),
        in_specs=[vmem, hbm, hbm],
        out_specs=(vmem, vmem),
        scratch_shapes=[
            pltpu.VMEM((n, F, R, M), LINK),
            pltpu.VMEM((n, T, M), jnp.bfloat16),
            pltpu.VMEM(previous.shape, jnp.float32),
            pltpu.VMEM(replicas.shape, jnp.bfloat16),
            pltpu.VMEM((M, n * T), jnp.float32),
            pltpu.VMEM((F, 256, M), jnp.bfloat16),
            pltpu.VMEM((F, 1, M), jnp.float32),
            pltpu.VMEM((F, cells, 128), jnp.float32),
            pltpu.VMEM((nf, 1, cells), jnp.float32),
            dma((F + 1, 3)), dma((F + 1, 2, chips)), dma((F + 1, 2, chips)),
            dma((F + 1, 2, chips)), dma((F + 1, 2, chips)),
            dma((nf,)), dma((nf,)), dma((F,)), dma,
        ],
        compiler_params=pltpu.CompilerParams(
            collective_id=0, has_side_effects=True, vmem_limit_bytes=48 * 1024 * 1024
        ),
    )(snapshots, pltpu.with_memory_space_constraint(previous, pltpu.HBM), pltpu.with_memory_space_constraint(replicas, pltpu.HBM))
    return (power.reshape(cells), csdm)


def solution(mesh):
    placed = (
        P("freq", None, "cell", None),
        P("freq", None, "cell", None),
        P("freq", None, "cell", None),
    )
    return jax.shard_map(
        on_device,
        mesh=mesh,
        in_specs=placed,
        out_specs=(P("cell"), P("freq", None, "cell", None)),
        check_vma=False,
    )
```
